32 devices in a mesh: rows: 4 (over x, core), cols: 8 (over z, y).
Axes of the slice: x: 2, y: 2, z: 4, core: 2. Of those that a mesh axis runs over, the one named last changes fastest.
Arguments:
- object_field: float32 [2, 1024, 2048], P(None, 'rows', 'cols'), may hold values from -4 to 4
- probe_modes: float32 [4, 2, 128, 128], replicated, may hold values from -2 to 2
- intensity: float32 [512, 128, 128], P(('rows', 'cols')), may hold values from 0.25 to 1.75
- positions: int32 [512, 2], P(('rows', 'cols')), may hold values from 0 to 256
- frame_count: int32 [32], P(('rows', 'cols')), may hold values from 1 to 16, as said below
Outputs:
- object_out: float32 [2, 1024, 2048], P(None, 'rows', 'cols')
- probe_out: float32 [4, 2, 128, 128], replicated
The draws below stay inside these ranges and needn't reach their ends.
Inputs may be any that keep to these rules, and one draw needn't show every extreme that they name: `frame_count`: some device has all 16 slots live.
All inputs are finite; a program needn't handle non-finite values.
Results may differ from the reference program's by a relative error of at most 0.0003.
Values sent between devices are 32-bit elements; how exact they have to be, the bound alone decides.
A program may use at most 128 MiB of HBM per device.

```python
import math
import jax
import jax.numpy as jnp
from jax import lax

W = 128
MODES = 4
HALF = 64
TILE = 256
FCAP = 16
ITERS = 2
FRAMES = 512
NY = 1024
NX = 2048
N_ROWS = 4
N_COLS = 8


def draw_frame_count(key, part):
    devices = N_ROWS * N_COLS
    first_key, second_key = jax.random.split(jax.random.fold_in(key, 17))
    counts = jax.random.randint(first_key, (devices,), 1, FCAP + 1)
    busiest = jax.random.randint(second_key, (), 0, devices)
    return jnp.where(jnp.arange(devices) == busiest, FCAP, counts).astype(jnp.int32)


def with_ends(result, own_key, low, top_value):
    index_at = [jax.random.randint(jax.random.fold_in(own_key, axis), (), 0, length) for axis, length in enumerate(result.shape)]
    longest = result.shape.index(max(result.shape))
    beside = index_at[:longest] + [(index_at[longest] + 1) % result.shape[longest]] + index_at[longest + 1:]
    return result.at[tuple(index_at)].set(low).at[tuple(beside)].set(top_value)


def steps_of(own_key, dims, cuts, low, high):
    level, own = 1.0, jax.random.fold_in(own_key, 6)
    for dim, blocks in cuts:
        steps = jnp.exp(jax.random.uniform(jax.random.fold_in(own, dim), (blocks,), jnp.float32, low / len(cuts), high / len(cuts)))
        level = level * jnp.repeat(steps, dims[dim] // blocks).reshape([-1 if axis == dim else 1 for axis in range(len(dims))])
    return level


def scatter_about(key, extent, spread, most, shards=(), kind=jnp.bfloat16):
    gain = steps_of(key, extent, shards, -0.22, 0.18) if shards else 1.0
    values = jax.random.normal(key, extent, jnp.float32) * spread * gain
    return jnp.minimum(jnp.maximum(values, -most), most).astype(kind)


def setup_inputs(seed: int = 0) -> dict:
    key_of = jax.random.split(jax.random.key(seed), 6)
    object_field = scatter_about(key_of[0], (2, NY, NX), 0.7, 4.0, ((1, 4), (2, 8)), jnp.float32)
    probe_modes = scatter_about(key_of[1], (MODES, 2, W, W), 0.35, 2.0, (), jnp.float32)
    intensity = jnp.clip(0.25 + 1.5 * jax.random.uniform(key_of[2], (FRAMES, W, W), jnp.float32) ** steps_of(key_of[2], (FRAMES, W, W), ((0, 32),), -0.2, 0.2), 0.25, 1.75)
    positions = with_ends(jax.random.randint(key_of[3], (FRAMES, 2), 0, TILE + 1), jax.random.fold_in(key_of[3], 1), 0, TILE).astype(jnp.int32)
    frame_count = draw_frame_count(jax.random.fold_in(key_of[5], 71), 0)
    return {"object_field": object_field, "probe_modes": probe_modes, "intensity": intensity, "positions": positions, "frame_count": frame_count}


object_rate = 0.1
probe_rate = 2.0


def transfer_phase(width):
    index = jnp.arange(width, dtype=jnp.int32)
    freq = jnp.where(index < width // 2, index, index - width).astype(jnp.float32)
    theta = math.pi * freq * freq / width
    total = theta[:, None] + theta[None, :]
    return jnp.cos(total) - 1j * jnp.sin(total)


def reference(object_field, probe_modes, intensity, positions, frame_count):
    obj = object_field[0] + 1j * object_field[1]
    prb = probe_modes[:, 0] + 1j * probe_modes[:, 1]
    phase = transfer_phase(W)
    for it in range(ITERS):
        padded = jnp.pad(obj, HALF)

        def step(frame, carry):
            gobj, gprb = carry
            frame = frame.astype(jnp.int32)
            device = frame // FCAP
            slot = frame % FCAP
            row0 = ((device // N_COLS) * TILE + positions[frame, 0]).astype(jnp.int32)
            col0 = ((device % N_COLS) * TILE + positions[frame, 1]).astype(jnp.int32)
            patch = lax.dynamic_slice(padded, (row0, col0), (W, W))
            live = (slot < frame_count[device]).astype(jnp.float32)
            wave = jnp.fft.ifft2(phase * jnp.fft.fft2(prb * patch[None]))
            inten = jnp.sum(jnp.real(wave) ** 2 + jnp.imag(wave) ** 2, axis=0)
            resid = (inten - intensity[frame]) * live
            back = jnp.fft.ifft2(jnp.conj(phase) * jnp.fft.fft2(4.0 * resid[None] * wave))
            gpatch = jnp.sum(jnp.conj(prb) * back, axis=0)
            gprb = gprb + jnp.conj(patch)[None] * back
            current = lax.dynamic_slice(gobj, (row0, col0), (W, W))
            gobj = lax.dynamic_update_slice(gobj, current + gpatch, (row0, col0))
            return gobj, gprb

        init = (jnp.zeros(padded.shape, padded.dtype), jnp.zeros(prb.shape, prb.dtype))
        gobj, gprb = lax.fori_loop(0, FRAMES, step, init)
        obj = obj - object_rate * gobj[HALF:HALF + NY, HALF:HALF + NX]
        prb = prb - (probe_rate / FRAMES) * gprb
    object_out = jnp.stack([jnp.real(obj), jnp.imag(obj)]).astype(jnp.float32)
    probe_out = jnp.stack([jnp.real(prb), jnp.imag(prb)], axis=1).astype(jnp.float32)
    return (object_out, probe_out)
```

```python
from functools import partial
import math

import jax
import jax.numpy as jnp
import numpy as np
from jax import lax
from jax.experimental import pallas as pl
from jax.experimental.pallas import tpu as pltpu
from jax.sharding import PartitionSpec as P

ITERS = 2
object_rate = 0.1
probe_rate = 2.0
f32 = jnp.float32
bf16 = jnp.bfloat16


def extended_2(cells, sides, width):
    for axis, dim in sides:
        count = lax.axis_size(axis)
        ends = count - 1
        head = lax.slice_in_dim(cells, 0, width, axis=dim)
        tail = lax.slice_in_dim(cells, cells.shape[dim] - width, cells.shape[dim], axis=dim)
        cells = jnp.concatenate(
            [
                lax.ppermute(tail, axis, [(i, (i + 1) % count) for i in range(ends)]),
                cells,
                lax.ppermute(head, axis, [((i + 1) % count, i) for i in range(ends)]),
            ],
            axis=dim,
        )
    return cells


def chirp(width):
    j = np.arange(width)
    turn = (j * j) % (2 * width)
    angle = math.pi * ((turn[:, None] + turn[None, :]) % (2 * width)) / width
    return np.cos(angle).astype(np.float32), np.sin(angle).astype(np.float32)


def split_np(matrix):
    high = matrix.astype(np.float32).astype(bf16)
    low = (matrix - high.astype(np.float64)).astype(np.float32).astype(bf16)
    return np.asarray(high), np.asarray(low)


def transforms(width):
    j = np.arange(width)
    angle = 2.0 * math.pi * ((j[:, None] * j[None, :]) % width) / width
    c, s = np.cos(angle) / math.sqrt(width), np.sin(angle) / math.sqrt(width)
    plus = np.block([[c, -s], [s, c]])
    minus = np.block([[c, s], [-s, c]])
    out = []
    for m in (plus, minus):
        high, low = split_np(m)
        out.append(np.concatenate([high, high, low], axis=0))
    for m in (minus, plus):
        high, low = split_np(m)
        out.append(np.concatenate([high, high, low], axis=1))
    return out


def split(x):
    high = x.astype(bf16)
    return high, (x - high.astype(f32)).astype(bf16)


def right(x, weights):
    high, low = split(x)
    return jnp.dot(
        jnp.concatenate([high, low, high], axis=1), weights, preferred_element_type=f32
    )


def left(weights, x):
    high, low = split(x)
    return jnp.dot(
        weights, jnp.concatenate([high, low, high], axis=0), preferred_element_type=f32
    )


def frames_kernel(
    modes, width, step, pos, count, ext, probe, inten, rf, ra, lf, la, gext, gprobe
):
    slots = inten.shape[0]
    tall = width + 8
    gext[...] = jnp.zeros_like(gext)
    gprobe[...] = jnp.zeros_like(gprobe)

    def place(frame):
        row = pos[frame, 0]
        col = pos[frame, 1]
        top = pl.multiple_of(jnp.minimum(row // 8, (ext.shape[1] - tall) // 8) * 8, 8)
        base = pl.multiple_of(jnp.minimum(col // width, 1) * width, width)
        return top, row - top, base, col - base

    def moved(x, by, axis):
        return pltpu.roll(x, jnp.where(by == 0, 0, x.shape[axis] - by), axis)

    def frame_gradient(frame):
        top, down, base, shift = place(frame)
        o_r, o_i = [
            moved(
                moved(ext[k, pl.ds(top, tall), pl.ds(base, 2 * width)], shift, 1)[:, :width],
                down,
                0,
            )[:width]
            for k in range(2)
        ]
        x = []
        for m in range(modes):
            p_r, p_i = probe[m, 0], probe[m, 1]
            x.append(jnp.concatenate([p_r * o_r - p_i * o_i, p_r * o_i + p_i * o_r], axis=1))
        z = right(jnp.concatenate(x, axis=0), rf[...])
        z = jnp.concatenate(
            [
                jnp.concatenate(
                    [z[m * width : (m + 1) * width, :width], z[m * width : (m + 1) * width, width:]],
                    axis=0,
                )
                for m in range(modes)
            ],
            axis=1,
        )
        y = left(lf[...], z)
        power = y * y
        total = power[:width] + power[width:]
        i_sum = sum(total[:, m * width : (m + 1) * width] for m in range(modes))
        live = jnp.where(frame < count[0], 4.0, 0.0).astype(f32)
        e = live * (i_sum - inten[frame])
        e = jnp.concatenate([e] * modes, axis=1)
        w = y * jnp.concatenate([e, e], axis=0)
        v = left(la[...], w)
        v = jnp.concatenate(
            [
                jnp.concatenate(
                    [v[:width, m * width : (m + 1) * width], v[width:, m * width : (m + 1) * width]],
                    axis=1,
                )
                for m in range(modes)
            ],
            axis=0,
        )
        d = right(v, ra[...])
        go_r = go_i = 0.0
        parts = []
        for m in range(modes):
            d_r = d[m * width : (m + 1) * width, :width]
            d_i = d[m * width : (m + 1) * width, width:]
            p_r, p_i = probe[m, 0], probe[m, 1]
            go_r += p_r * d_r + p_i * d_i
            go_i += p_r * d_i - p_i * d_r
            parts.append((o_r * d_r + o_i * d_i, o_r * d_i - o_i * d_r))
        return (go_r, go_i), parts

    def body(block, carry):
        frames = [block * step + k for k in range(step)]
        results = [frame_gradient(frame) for frame in frames]
        for m in range(modes):
            for k in range(2):
                gprobe[m, k] += sum(parts[m][k] for _, parts in results)
        for frame, (grad, _) in zip(frames, results):
            top, down, base, shift = place(frame)
            for k in range(2):
                wide = jnp.concatenate([grad[k], jnp.zeros((8, width), f32)], axis=0)
                wide = pltpu.roll(wide, down, 0)
                wide = jnp.concatenate([wide, jnp.zeros_like(wide)], axis=1)
                wide = pltpu.roll(wide, shift, 1)
                where = (k, pl.ds(top, tall), pl.ds(base, 2 * width))
                gext[where] += wide
        return carry

    lax.fori_loop(0, slots // step, body, 0)


def frame_pass(extended, probe, positions, intensity, count, step=4):
    modes, _, width, _ = probe.shape
    weights = [jnp.asarray(w) for w in transforms(width)]
    vmem = pl.BlockSpec(memory_space=pltpu.VMEM)
    smem = pl.BlockSpec(memory_space=pltpu.SMEM)
    slots = intensity.shape[0]
    return pl.pallas_call(
        partial(frames_kernel, modes, width, step),
        out_shape=(
            jax.ShapeDtypeStruct(extended.shape, f32),
            jax.ShapeDtypeStruct(probe.shape, f32),
        ),
        in_specs=[smem, smem] + [vmem] * 7,
        out_specs=(vmem, vmem),
        compiler_params=pltpu.CompilerParams(vmem_limit_bytes=48 * 1024 * 1024),
        cost_estimate=pl.CostEstimate(
            flops=slots * modes * 4 * 3 * 2 * width * 4 * width * width,
            bytes_accessed=4 * (extended.size * 2 + probe.size * 2 + intensity.size),
            transcendentals=0,
        ),
    )(positions, count, extended, probe, intensity, *weights)


def fold_rims(padded, dim, start, length, width):
    total = padded.shape[dim]
    core = lax.slice_in_dim(padded, start, start + length, axis=dim)
    low = lax.slice_in_dim(padded, 0, width, axis=dim)
    high = lax.slice_in_dim(padded, total - width, total, axis=dim)
    low_pad = [(0, 0)] * padded.ndim
    high_pad = [(0, 0)] * padded.ndim
    low_pad[dim] = (0, length - width)
    high_pad[dim] = (length - width, 0)
    return core + jnp.pad(low, low_pad) + jnp.pad(high, high_pad)


SIDES = (("rows", 1), ("cols", 2))


def return_gradient(gext, tile, width, half):
    padded = extended_2(gext, SIDES, half)
    folded = fold_rims(padded, 1, width, tile, half)
    return fold_rims(folded, 2, width, tile, half)


def times(field, c_real, c_imag):
    real, imag = field[:, 0], field[:, 1]
    return jnp.stack([real * c_real - imag * c_imag, real * c_imag + imag * c_real], axis=1)


def body(object_field, probe_modes, intensity, positions, frame_count):
    tile = object_field.shape[1]
    width = probe_modes.shape[-1]
    half = width // 2
    slots = positions.shape[0]
    row_count = lax.axis_size("rows")
    col_count = lax.axis_size("cols")
    frames_all = slots * row_count * col_count
    c_real, c_imag = chirp(width)
    probe = times(probe_modes, c_real, c_imag)
    tile_field = object_field
    extended = extended_2(tile_field, SIDES, half)
    for it in range(ITERS):
        last = it == ITERS - 1
        gext, gprobe = frame_pass(extended, probe, positions, intensity, frame_count)
        total = lax.psum(gprobe, ("rows", "cols"))
        probe = probe - probe_rate / frames_all * total
        gradient = return_gradient(gext, tile, width, half)
        tile_field = tile_field - object_rate * gradient
        if not last:
            extended = extended_2(tile_field, SIDES, half)
    return (tile_field, times(probe, c_real, -c_imag))


def solution(mesh):
    return jax.shard_map(
        body,
        mesh=mesh,
        in_specs=(
            P(None, "rows", "cols"),
            P(),
            P(("rows", "cols"), None, None),
            P(("rows", "cols"), None),
            P(("rows", "cols")),
        ),
        out_specs=(P(None, "rows", "cols"), P()),
        check_vma=False,
    )
```

```python
from functools import partial
import math

import jax
import jax.numpy as jnp
import numpy as np
from jax import lax
from jax.experimental import pallas as pl
from jax.experimental.pallas import tpu as pltpu
from jax.sharding import PartitionSpec as P

ITERS = 2
object_rate = 0.1
probe_rate = 2.0
f32 = jnp.float32
bf16 = jnp.bfloat16


def chirp(width):
    j = np.arange(width)
    turn = (j * j) % (2 * width)
    angle = math.pi * ((turn[:, None] + turn[None, :]) % (2 * width)) / width
    return np.cos(angle).astype(np.float32), np.sin(angle).astype(np.float32)


def split_np(matrix):
    high = matrix.astype(np.float32).astype(bf16)
    low = (matrix - high.astype(np.float64)).astype(np.float32).astype(bf16)
    return np.asarray(high), np.asarray(low)


def transforms(width):
    j = np.arange(width)
    angle = 2.0 * math.pi * ((j[:, None] * j[None, :]) % width) / width
    c, s = np.cos(angle) / math.sqrt(width), np.sin(angle) / math.sqrt(width)
    plus = np.block([[c, -s], [s, c]])
    minus = np.block([[c, s], [-s, c]])
    out = []
    for m in (plus, minus):
        high, low = split_np(m)
        out.append(np.concatenate([high, high, low], axis=0))
    for m in (minus, plus):
        high, low = split_np(m)
        out.append(np.concatenate([high, high, low], axis=1))
    return out


def split(x):
    high = x.astype(bf16)
    return high, (x - high.astype(f32)).astype(bf16)


def right(x, weights):
    high, low = split(x)
    return jnp.dot(
        jnp.concatenate([high, low, high], axis=1), weights, preferred_element_type=f32
    )


def left(weights, x):
    high, low = split(x)
    return jnp.dot(
        weights, jnp.concatenate([high, low, high], axis=0), preferred_element_type=f32
    )


def frames_kernel(
    modes, width, step, pos, count, ext, probe, inten, rf, ra, lf, la, gext, gprobe
):
    slots = inten.shape[0]
    tall = width + 8
    gext[...] = jnp.zeros_like(gext)
    gprobe[...] = jnp.zeros_like(gprobe)

    def place(frame):
        row = pos[frame, 0]
        col = pos[frame, 1]
        top = pl.multiple_of(jnp.minimum(row // 8, (ext.shape[1] - tall) // 8) * 8, 8)
        base = pl.multiple_of(jnp.minimum(col // width, 1) * width, width)
        return top, row - top, base, col - base

    def moved(x, by, axis):
        return pltpu.roll(x, jnp.where(by == 0, 0, x.shape[axis] - by), axis)

    def frame_gradient(frame):
        top, down, base, shift = place(frame)
        o_r, o_i = [
            moved(
                moved(ext[k, pl.ds(top, tall), pl.ds(base, 2 * width)], shift, 1)[:, :width],
                down,
                0,
            )[:width]
            for k in range(2)
        ]
        x = []
        for m in range(modes):
            p_r, p_i = probe[m, 0], probe[m, 1]
            x.append(jnp.concatenate([p_r * o_r - p_i * o_i, p_r * o_i + p_i * o_r], axis=1))
        z = right(jnp.concatenate(x, axis=0), rf[...])
        z = jnp.concatenate(
            [
                jnp.concatenate(
                    [z[m * width : (m + 1) * width, :width], z[m * width : (m + 1) * width, width:]],
                    axis=0,
                )
                for m in range(modes)
            ],
            axis=1,
        )
        y = left(lf[...], z)
        power = y * y
        total = power[:width] + power[width:]
        i_sum = sum(total[:, m * width : (m + 1) * width] for m in range(modes))
        live = jnp.where(frame < count[0], 4.0, 0.0).astype(f32)
        e = live * (i_sum - inten[frame])
        e = jnp.concatenate([e] * modes, axis=1)
        w = y * jnp.concatenate([e, e], axis=0)
        v = left(la[...], w)
        v = jnp.concatenate(
            [
                jnp.concatenate(
                    [v[:width, m * width : (m + 1) * width], v[width:, m * width : (m + 1) * width]],
                    axis=1,
                )
                for m in range(modes)
            ],
            axis=0,
        )
        d = right(v, ra[...])
        go_r = go_i = 0.0
        parts = []
        for m in range(modes):
            d_r = d[m * width : (m + 1) * width, :width]
            d_i = d[m * width : (m + 1) * width, width:]
            p_r, p_i = probe[m, 0], probe[m, 1]
            go_r += p_r * d_r + p_i * d_i
            go_i += p_r * d_i - p_i * d_r
            parts.append((o_r * d_r + o_i * d_i, o_r * d_i - o_i * d_r))
        return (go_r, go_i), parts

    def body(block, carry):
        frames = [block * step + k for k in range(step)]
        results = [frame_gradient(frame) for frame in frames]
        for m in range(modes):
            for k in range(2):
                gprobe[m, k] += sum(parts[m][k] for _, parts in results)
        for frame, (grad, _) in zip(frames, results):
            top, down, base, shift = place(frame)
            for k in range(2):
                wide = jnp.concatenate([grad[k], jnp.zeros((8, width), f32)], axis=0)
                wide = pltpu.roll(wide, down, 0)
                wide = jnp.concatenate([wide, jnp.zeros_like(wide)], axis=1)
                wide = pltpu.roll(wide, shift, 1)
                where = (k, pl.ds(top, tall), pl.ds(base, 2 * width))
                gext[where] += wide
        return carry

    lax.fori_loop(0, slots // step, body, 0)


def frame_pass(extended, probe, positions, intensity, count, step=8):
    modes, _, width, _ = probe.shape
    weights = [jnp.asarray(w) for w in transforms(width)]
    vmem = pl.BlockSpec(memory_space=pltpu.VMEM)
    smem = pl.BlockSpec(memory_space=pltpu.SMEM)
    slots = intensity.shape[0]
    step = math.gcd(step, slots)
    return pl.pallas_call(
        partial(frames_kernel, modes, width, step),
        out_shape=(
            jax.ShapeDtypeStruct(extended.shape, f32),
            jax.ShapeDtypeStruct(probe.shape, f32),
        ),
        in_specs=[smem, smem] + [vmem] * 7,
        out_specs=(vmem, vmem),
        compiler_params=pltpu.CompilerParams(vmem_limit_bytes=48 * 1024 * 1024),
        cost_estimate=pl.CostEstimate(
            flops=slots * modes * 4 * 3 * 2 * width * 4 * width * width,
            bytes_accessed=4 * (extended.size * 2 + probe.size * 2 + intensity.size),
            transcendentals=0,
        ),
    )(positions, count, extended, probe, intensity, *weights)


MESH = pl.DeviceIdType.MESH


def packed(rim):
    rows = rim.shape[1] // 2
    return jnp.concatenate([rim[:, :rows], rim[:, rows:]], axis=2)


def unpacked(block):
    half = block.shape[2] // 2
    return jnp.concatenate([block[:, :, :half], block[:, :, half:]], axis=1)


def exchange_kernel(sizes, reduce, give, fetch, names, *refs):
    n_rows, n_cols, n_z, tile, half, rate = sizes
    ref = dict(zip(names, refs))
    row, col = lax.axis_index("rows"), lax.axis_index("cols")
    core, chip_x = lax.rem(row, 2), row // 2
    n_y = n_cols // n_z
    chip_y, chip_z = lax.rem(col, n_y), col // n_y
    n_b = (n_rows // 2) * n_y
    place_b = chip_x * n_y + chip_y

    def peers_core():
        return [(1, 1 - core, (chip_x * 2 + 1 - core, col))]

    def peers_b():
        out = []
        for k in range(1, n_b):
            b = lax.rem(place_b + k, n_b)
            out.append((k, b, ((b // n_y) * 2 + core, chip_z * n_y + lax.rem(b, n_y))))
        return out

    def peers_z():
        out = []
        for k in range(1, n_z):
            z = lax.rem(chip_z + k, n_z)
            out.append((k, z, (row, z * n_y + chip_y)))
        return out

    sides = {
        "rows": ((row > 0, (row - 1, col)), (row < n_rows - 1, (row + 1, col))),
        "cols": ((col > 0, (row, col - 1)), (col < n_cols - 1, (row, col + 1))),
    }

    barrier = pltpu.get_barrier_semaphore()
    fixed = peers_core() + peers_b() + peers_z() if reduce else []
    for _, _, device in fixed:
        pl.semaphore_signal(barrier, inc=1, device_id=device, device_id_type=MESH)
    for pair in sides.values():
        for there, device in pair:

            @pl.when(there)
            def _():
                pl.semaphore_signal(barrier, inc=1, device_id=device, device_id_type=MESH)

    beside = sum(there.astype(jnp.int32) for pair in sides.values() for there, _ in pair)
    pl.semaphore_wait(barrier, beside + len(fixed))

    def sum_probe():
        grad, full, acc = ref["gprobe"], ref["full"], ref["acc"]
        size_core = grad.shape[0] // 2
        size_b = size_core // n_b
        size_z = size_b // n_z
        send, recv = ref["r_send"], ref["r_recv"]
        counter = [0]

        def at(start, size):
            return pl.ds(pl.multiple_of(start, 8), size)

        def begin(peers, src_of, dst_of):
            copies = []
            for k, which, device in peers:
                copy = pltpu.make_async_remote_copy(
                    src_ref=src_of(which),
                    dst_ref=dst_of(k),
                    send_sem=send.at[counter[0]],
                    recv_sem=recv.at[counter[0]],
                    device_id=device,
                    device_id_type=MESH,
                )
                counter[0] += 1
                copy.start()
                copies.append(copy)
            return copies

        base_core = core * size_core
        base_b = base_core + place_b * size_b
        base_z = base_b + chip_z * size_z
        in_core, in_b, in_z = ref["in_core"], ref["in_b"], ref["in_z"]
        stages = (
            (peers_core(), grad, 0, size_core, base_core, in_core),
            (peers_b(), acc, base_core, size_b, base_b, in_b),
            (peers_z(), acc, base_b, size_z, base_z, in_z),
        )
        for peers, source, start, size, mine, landing in stages:
            copies = begin(
                peers,
                lambda which: source.at[at(start + which * size, size)],
                lambda k: landing.at[k - 1],
            )
            yield
            for copy in copies:
                copy.wait()
            value = source[at(mine, size)]
            for k in range(len(peers)):
                value = value + landing[k]
            target = full if landing is in_z else acc
            target[at(mine, size)] = value
        for peers, _, _, size, mine, _ in reversed(stages):
            copies = begin(
                peers, lambda which: full.at[at(mine, size)], lambda k: full.at[at(mine, size)]
            )
            yield
            for copy in copies:
                copy.wait()
        ref["probe_out"][...] = ref["probe"][...] - rate * full[...]

    def swap(side, tag, low, high):
        (has_low, low_device), (has_high, high_device) = sides[side]
        from_low, from_high = ref[tag + "_low"], ref[tag + "_high"]
        sems = ref[tag + "_sems"]
        to_low = pltpu.make_async_remote_copy(
            low, from_high, sems.at[0], sems.at[1], device_id=low_device, device_id_type=MESH
        )
        to_high = pltpu.make_async_remote_copy(
            high, from_low, sems.at[2], sems.at[3], device_id=high_device, device_id_type=MESH
        )

        @pl.when(has_low)
        def _():
            to_low.start()

        @pl.when(has_high)
        def _():
            to_high.start()

        yield

        @pl.when(has_low)
        def _():
            to_low.wait_send()
            to_high.wait_recv()

        @pl.when(jnp.logical_not(has_low))
        def _():
            from_low[...] = jnp.zeros_like(from_low)

        @pl.when(has_high)
        def _():
            to_high.wait_send()
            to_low.wait_recv()

        @pl.when(jnp.logical_not(has_high))
        def _():
            from_high[...] = jnp.zeros_like(from_high)

    def together(*parts):
        for part in parts:
            next(part)
        yield
        for part in parts:
            next(part, None)

    def move_object():
        end = tile + half
        inner = tile - 2 * half
        if give:
            gext = ref["gext"]
            ref["b_to"][0] = packed(gext[:, half:end, :half])
            ref["b_to"][1] = packed(gext[:, half:end, end:])
            yield from together(
                swap("rows", "a", gext.at[:, pl.ds(0, half), :], gext.at[:, pl.ds(end, half), :]),
                swap("cols", "b", ref["b_to"].at[0], ref["b_to"].at[1]),
            )
            a_low, a_high = ref["a_low"][...], ref["a_high"][...]
            ref["e_to"][0] = jnp.concatenate([a_low[:, :, :half], a_high[:, :, :half]], axis=2)
            ref["e_to"][1] = jnp.concatenate([a_low[:, :, end:], a_high[:, :, end:]], axis=2)
            yield from swap("cols", "e", ref["e_to"].at[0], ref["e_to"].at[1])
            beside = []
            for name in ("low", "high"):
                corner = ref["e_" + name][...]
                beside.append(
                    unpacked(ref["b_" + name][...])
                    + jnp.concatenate(
                        [corner[:, :, :half], jnp.zeros((2, inner, half), f32), corner[:, :, half:]],
                        axis=1,
                    )
                )
            across = jnp.concatenate(
                [beside[0], jnp.zeros((2, tile, inner), f32), beside[1]], axis=2
            )
            down = jnp.concatenate(
                [a_low[:, :, half:end], jnp.zeros((2, inner, tile), f32), a_high[:, :, half:end]],
                axis=1,
            )
            grad = gext[:, half:end, half:end] + across + down
            old = ref["field"][:, half:end, half:end]
            cells = ref["cells"]
            cells[...] = old - object_rate * grad
        else:
            cells = ref["field"]
        if fetch:
            ref["d_to"][0] = packed(cells[:, :, :half])
            ref["d_to"][1] = packed(cells[:, :, tile - half :])
            yield from together(
                swap(
                    "rows",
                    "c",
                    cells.at[:, pl.ds(0, half), :],
                    cells.at[:, pl.ds(tile - half, half), :],
                ),
                swap("cols", "d", ref["d_to"].at[0], ref["d_to"].at[1]),
            )
            low, high = unpacked(ref["d_low"][...]), unpacked(ref["d_high"][...])
            ref["f_to"][0] = jnp.concatenate([low[:, :half], high[:, :half]], axis=2)
            ref["f_to"][1] = jnp.concatenate([low[:, tile - half :], high[:, tile - half :]], axis=2)
            yield from swap("rows", "f", ref["f_to"].at[0], ref["f_to"].at[1])
            ext = ref["ext"]
            ext[:, half:end, :] = jnp.concatenate([low, cells[...], high], axis=2)
            for name, start in (("low", 0), ("high", end)):
                corner = ref["f_" + name][...]
                ext[:, start : start + half, :] = jnp.concatenate(
                    [corner[:, :, :half], ref["c_" + name][...], corner[:, :, half:]], axis=2
                )

    todo = ([sum_probe()] if reduce else []) + [move_object()]
    while todo:
        todo = [part for part in todo if next(part, 0) is None]


def exchange(ident, tile, half, slots, field, gext=None, gprobe=None, probe=None, fetch=True):
    reduce = give = gext is not None
    n_rows, n_cols = lax.axis_size("rows"), lax.axis_size("cols")
    n_z = 4 if n_cols % 4 == 0 else 1
    n_b = (n_rows // 2) * (n_cols // n_z)
    wide = tile + 2 * half
    vm = lambda *shape: pltpu.VMEM(shape, f32)
    dma = lambda n: pltpu.SemaphoreType.DMA((n,))
    names, ops, outs, out_names, scratch = ["field"], [field], [], [], {}
    shape = None
    if reduce:
        shape = probe.shape
        width = shape[-1]
        rows = probe.size // width
        names += ["gext", "gprobe", "probe"]
        ops += [gext, gprobe.reshape(rows, width), probe.reshape(rows, width)]
        core = rows // 2
        count = 2 * (1 + n_b - 1 + n_z - 1)
        scratch |= {
            "full": vm(rows, width),
            "acc": vm(rows, width),
            "in_core": vm(1, core, width),
            "in_b": vm(max(n_b - 1, 1), core // n_b, width),
            "in_z": vm(max(n_z - 1, 1), core // n_b // n_z, width),
            "r_send": dma(count),
            "r_recv": dma(count),
        }

    def lands(tag, *size):
        return {tag + "_low": vm(*size), tag + "_high": vm(*size), tag + "_sems": dma(4)}

    if give:
        scratch |= lands("a", 2, half, wide)
        scratch |= lands("b", 2, tile // 2, 2 * half)
        scratch |= lands("e", 2, half, 2 * half)
        scratch["b_to"] = vm(2, 2, tile // 2, 2 * half)
        scratch["e_to"] = vm(2, 2, half, 2 * half)
    if fetch:
        scratch |= lands("c", 2, half, tile)
        scratch |= lands("d", 2, tile // 2, 2 * half)
        scratch |= lands("f", 2, half, 2 * half)
        scratch["d_to"] = vm(2, 2, tile // 2, 2 * half)
        scratch["f_to"] = vm(2, 2, half, 2 * half)
        outs.append(jax.ShapeDtypeStruct((2, wide, wide), f32))
        out_names.append("ext")
        if give:
            scratch["cells"] = vm(2, tile, tile)
    else:
        outs.append(jax.ShapeDtypeStruct((2, tile, tile), f32))
        out_names.append("cells")
    if reduce:
        outs.append(jax.ShapeDtypeStruct((rows, width), f32))
        out_names.append("probe_out")
        rate = probe_rate / (n_rows * n_cols * slots)
    else:
        rate = 0.0
    vmem = pl.BlockSpec(memory_space=pltpu.VMEM)
    out = pl.pallas_call(
        partial(
            exchange_kernel,
            (n_rows, n_cols, n_z, tile, half, rate),
            reduce,
            give,
            fetch,
            names + out_names + list(scratch),
        ),
        out_shape=tuple(outs),
        in_specs=[vmem] * len(ops),
        out_specs=tuple([vmem] * len(outs)),
        scratch_shapes=list(scratch.values()),
        compiler_params=pltpu.CompilerParams(
            collective_id=ident, has_side_effects=True, vmem_limit_bytes=48 * 1024 * 1024
        ),
    )(*ops)
    return out[0], (out[1].reshape(shape) if reduce else None)


def times(field, c_real, c_imag):
    real, imag = field[:, 0], field[:, 1]
    return jnp.stack([real * c_real - imag * c_imag, real * c_imag + imag * c_real], axis=1)


def body(object_field, probe_modes, intensity, positions, frame_count):
    tile = object_field.shape[1]
    width = probe_modes.shape[-1]
    half = width // 2
    slots = positions.shape[0]
    c_real, c_imag = chirp(width)
    probe = times(probe_modes, c_real, c_imag)
    field, _ = exchange(0, tile, half, slots, object_field)
    for it in range(ITERS):
        gext, gprobe = frame_pass(field, probe, positions, intensity, frame_count)
        field, probe = exchange(
            it + 1, tile, half, slots, field, gext, gprobe, probe, fetch=it < ITERS - 1
        )
    return (field, times(probe, c_real, -c_imag))


def solution(mesh):
    return jax.shard_map(
        body,
        mesh=mesh,
        in_specs=(
            P(None, "rows", "cols"),
            P(),
            P(("rows", "cols"), None, None),
            P(("rows", "cols"), None),
            P(("rows", "cols")),
        ),
        out_specs=(P(None, "rows", "cols"), P()),
        check_vma=False,
    )
```
